32 devices in a mesh: lat: 2 (over y), comp: 16 (over z, x, core).
Axes of the slice: x: 2, y: 2, z: 4, core: 2. Of those that a mesh axis runs over, the one named last changes fastest.
Arguments:
- spectrum: float32 [1152, 32, 1024], P('comp', 'lat'), may hold values from -4 to 4
- interp_plus: float32 [1152, 1152], P('lat'), may hold values from -0.1875 to 0.1875
- interp_minus: float32 [1152, 1152], P('lat'), may hold values from -0.1875 to 0.1875
- source_gain: float32 [1152], replicated, may hold values from 0.05 to 0.3
- current: float32 [2, 32, 1024], P(None, 'lat'), may hold values from -0.2 to 0.2
- sea_mask: int32 [32, 1024], P('lat'), may hold values 0 or 1
- limiter_flags: int32 [32, 1024], P('lat'), may hold values 0 or 1
- ice_cells: int32 [1024], replicated, may hold values from 0 to 32767
Outputs:
- spectrum_out: float32 [1152, 32, 1024], P('comp', 'lat')
The draws below stay inside these ranges and needn't reach their ends.
Inputs may be any that keep to these rules, and one draw needn't show every extreme that they name: `ice_cells`: indices may repeat.
All inputs are finite; a program needn't handle non-finite values. No bound on the sum of `sea_mask` or of `limiter_flags` on one device may be relied on, other than what follows from the above.
Results may differ from the reference program's by a relative error of at most 0.0003.
Values sent between devices are 32-bit elements; how exact they have to be, the bound alone decides.
A program may use at most 128 MiB of HBM per device.

```python
import math
import jax
import jax.numpy as jnp
from jax import lax

ND = 36
NF = 32
K = 1152
NLON = 1024
NLAT = 32
OUTER = 2
SUB = 2
NICE = 1024


def plant(drawn, key, smallest, high):
    spot = [jax.random.randint(jax.random.fold_in(key, axis), (), 0, length) for axis, length in enumerate(drawn.shape)]
    main_axis = drawn.shape.index(max(drawn.shape))
    neighbour = spot[:main_axis] + [(spot[main_axis] + 1) % drawn.shape[main_axis]] + spot[main_axis + 1:]
    return drawn.at[tuple(spot)].set(smallest).at[tuple(neighbour)].set(high)


def level_of(key, dims, pieces, smallest, high):
    level = 1.0
    for dim, shards_of in pieces:
        draws = jax.random.uniform(jax.random.fold_in(jax.random.fold_in(key, 6), dim), (shards_of,), jnp.float32, smallest / len(pieces), high / len(pieces))
        level = level * jnp.repeat(jnp.exp(draws), dims[dim] // shards_of).reshape((-1,) + (1,) * (len(dims) - 1 - dim))
    return level


def gaussian(stream_key, extent, spread, reach, split=(), kind=jnp.bfloat16):
    entries = jax.random.normal(stream_key, extent, jnp.float32) * spread
    if len(split) > 0:
        entries = level_of(stream_key, extent, split, -0.22, 0.18) * entries
    return jnp.clip(entries, min=-reach, max=reach).astype(kind)


def setup_inputs(seed: int = 0) -> dict:
    arg_keys = jax.random.split(jax.random.key(seed), 9)
    spectrum = gaussian(arg_keys[0], (K, NLAT, NLON), 1.0, 4.0, ((0, 16), (1, 2)), jnp.float32)
    interp_plus = gaussian(arg_keys[1], (K, K), K ** -0.5, 0.1875, ((0, 2),), jnp.float32)
    interp_minus = gaussian(arg_keys[2], (K, K), K ** -0.5, 0.1875, ((0, 2),), jnp.float32)
    source_gain = jnp.clip(jnp.exp(jax.random.uniform(arg_keys[3], (K,), jnp.float32, math.log(0.05), math.log(0.3))), 0.05, 0.3)
    current = jnp.clip(jax.random.uniform(arg_keys[4], (2, NLAT, NLON), jnp.float32, -0.2, 0.2) * level_of(arg_keys[4], (2, NLAT, NLON), ((1, 2),), -0.4, 0.0), -0.2, 0.2)
    sea_mask = plant((jax.random.randint(arg_keys[5], (NLAT, NLON), 0, 5) < 4).astype(jnp.int32), jax.random.fold_in(arg_keys[5], 1), 0, 1)
    limiter_flags = plant((jax.random.randint(arg_keys[6], (NLAT, NLON), 0, 2) < 1).astype(jnp.int32), jax.random.fold_in(arg_keys[6], 1), 0, 1)
    ice_cells = plant(jax.random.randint(arg_keys[7], (NICE,), 0, NLAT * NLON), jax.random.fold_in(arg_keys[7], 1), 0, (NLAT * NLON) - 1).astype(jnp.int32)
    return dict(spectrum=spectrum, interp_plus=interp_plus, interp_minus=interp_minus, source_gain=source_gain, current=current, sea_mask=sea_mask, limiter_flags=limiter_flags, ice_cells=ice_cells)


def minmod(first, second):
    return 0.5 * (jnp.sign(first) + jnp.sign(second)) * jnp.minimum(jnp.abs(first), jnp.abs(second))


def speeds(index):
    direction = (index // NF).astype(jnp.float32)
    frequency = (index % NF).astype(jnp.float32)
    angle_dir = 2.0 * jnp.pi * (direction + 0.5) / ND
    magnitude = 0.35 * (0.5 + 0.5 * frequency / (NF - 1))
    return (magnitude * jnp.cos(angle_dir))[:, None, None], (magnitude * jnp.sin(angle_dir))[:, None, None]


def advect(padded, statics, speed_x, speed_y):
    centre = padded[:, 1:-1]
    drift_x = statics[0]
    drift_y = statics[1]
    flagged = statics[2]
    wet = statics[3]
    east = jnp.roll(centre, -1, axis=2)
    west = jnp.roll(centre, 1, axis=2)
    slope_x = flagged * minmod(east - centre, centre - west)
    face_x = speed_x + 0.5 * (drift_x + jnp.roll(drift_x, -1, axis=1))
    flux_x = jnp.where(face_x >= 0.0, face_x * (centre + 0.5 * (1.0 - face_x) * slope_x),
                       face_x * (east - 0.5 * (1.0 + face_x) * jnp.roll(slope_x, -1, axis=2)))
    change_x = flux_x - jnp.roll(flux_x, 1, axis=2)
    slope_y = flagged * minmod(padded[:, 2:] - centre, centre - padded[:, :-2])
    face_y = speed_y + 0.5 * (drift_y[:-1] + drift_y[1:])
    flux_y = jnp.where(face_y >= 0.0, face_y * (centre[:, :-1] + 0.5 * (1.0 - face_y) * slope_y[:, :-1]),
                       face_y * (centre[:, 1:] - 0.5 * (1.0 + face_y) * slope_y[:, 1:]))
    change_y = flux_y[:, 1:] - flux_y[:, :-1]
    return wet[1:-1] * (centre[:, 1:-1] - change_x[:, 1:-1] - change_y)


def quartet(field, plus, minus, gain_col, keep):
    forcing = field * field * (plus + minus) - 2.0 * field * plus * minus
    update = gain_col * forcing / (1.0 + gain_col * (plus * plus + minus * minus))
    return (field + update) * keep


def reference(spectrum, interp_plus, interp_minus, source_gain, current, sea_mask, limiter_flags, ice_cells):
    statics = jnp.stack([current[0], current[1], limiter_flags.astype(jnp.float32), sea_mask.astype(jnp.float32)])
    statics = jnp.pad(statics, ((0, 0), (1, 1), (0, 0)))
    speed_x, speed_y = speeds(jnp.arange(K, dtype=jnp.int32))
    iced = jnp.zeros((NLAT * NLON,), jnp.float32).at[ice_cells].set(1.0)
    keep = (1.0 - 0.6 * iced).reshape(NLAT, 1, NLON)
    gain_col = source_gain[:, None]

    def advect_block(items):
        block, block_x, block_y = items
        padded = jnp.pad(block, ((0, 0), (2, 2), (0, 0)))
        return advect(padded, statics, block_x, block_y)

    def source_row(items):
        row_field, kept = items
        plus = jnp.dot(interp_plus, row_field, precision=lax.Precision.HIGHEST, preferred_element_type=jnp.float32)
        minus = jnp.dot(interp_minus, row_field, precision=lax.Precision.HIGHEST, preferred_element_type=jnp.float32)
        return quartet(row_field, plus, minus, gain_col, kept)

    field = spectrum
    for outer_step in range(OUTER):
        for sub_step in range(SUB):
            blocks = lax.map(advect_block, (field.reshape(ND, NF, NLAT, NLON),
                                            speed_x.reshape(ND, NF, 1, 1), speed_y.reshape(ND, NF, 1, 1)))
            field = blocks.reshape(K, NLAT, NLON)
        rows_first = jnp.transpose(field, (1, 0, 2))
        field = jnp.transpose(lax.map(source_row, (rows_first, keep)), (1, 0, 2))
    return field
```

```python
import functools

import jax
import jax.numpy as jnp
from jax import lax
from jax.experimental import pallas as pl
from jax.experimental.pallas import tpu as pltpu
from jax.sharding import PartitionSpec as P

ND = 36
NF = 32
OUTER = 2
SUB = 2
HALO = 2 * SUB
LANES = 128
BOTH = ("lat", "comp")


def speeds(index):
    direction = (index // NF).astype(jnp.float32)
    frequency = (index % NF).astype(jnp.float32)
    angle_dir = 2.0 * jnp.pi * (direction + 0.5) / ND
    magnitude = 0.35 * (0.5 + 0.5 * frequency / (NF - 1))
    return (magnitude * jnp.cos(angle_dir))[None, :], (magnitude * jnp.sin(angle_dir))[None, :]


def minmod(first, second):
    return jnp.maximum(jnp.minimum(first, second), 0.0) + jnp.minimum(jnp.maximum(first, second), 0.0)


def upwind(face, low, low_slope, high, high_slope):
    half = 0.5 - 0.5 * jnp.abs(face)
    return face * jnp.where(face >= 0.0, low + half * low_slope, high - half * high_slope)


def advect_kernel(
    cx_ref, cy_ref, uf_ref, vf_ref, flag_ref, sea_ref, field_ref, left_ref, right_ref, out_ref, first, second
):
    rows, lons, lanes = field_ref.shape
    wide = lons + 2 * HALO
    zero = jnp.zeros((wide, lanes), jnp.float32)
    first[:rows, :HALO, :] = left_ref[...]
    first[:rows, HALO : HALO + lons, :] = field_ref[...]
    first[:rows, HALO + lons :, :] = right_ref[...]
    for extra in range(2):
        first[rows + extra] = zero
        second[rows + extra] = zero
    speed_x = cx_ref[...]
    speed_y = cy_ref[...]

    def substep(source, store):
        top = source[0]
        below = source[1]
        step = below - top
        slope = flag_ref[0] * minmod(step, top)
        flux = upwind(speed_y + vf_ref[0], zero, zero, top, slope)

        def row(r, carry):
            here, south, step, slope, flux = carry
            beyond = source[r + 2]
            next_step = beyond - south
            next_slope = flag_ref[r + 1] * minmod(next_step, step)
            next_flux = upwind(speed_y + vf_ref[r + 1], here, slope, south, next_slope)
            east = pltpu.roll(here, wide - 1, 0)
            forward = east - here
            slope_x = flag_ref[r] * minmod(forward, pltpu.roll(forward, 1, 0))
            flux_x = upwind(
                speed_x + uf_ref[r], here, slope_x, east, pltpu.roll(slope_x, wide - 1, 0)
            )
            change_x = flux_x - pltpu.roll(flux_x, 1, 0)
            store(r, sea_ref[r] * (here - change_x - (next_flux - flux)))
            return south, beyond, next_step, next_slope, next_flux

        lax.fori_loop(0, rows, row, (top, below, step, slope, flux), unroll=2)

    def keep_second(r, value):
        second[r] = value

    def keep_out(r, value):
        out_ref[r] = value[HALO : HALO + lons]

    substep(first, keep_second)
    substep(second, keep_out)


def advect(field, left, right, fixed):
    speed_x, speed_y, face_u, face_v, flag, sea = fixed
    rows, lons, comps = field.shape
    wide = lons + 2 * HALO
    column = lambda height: pl.BlockSpec((rows, height, LANES), lambda k: (0, 0, k))
    whole = lambda array: pl.BlockSpec(array.shape, lambda k: (0, 0, 0))
    return pl.pallas_call(
        advect_kernel,
        grid=(comps // LANES,),
        out_shape=jax.ShapeDtypeStruct(field.shape, jnp.float32),
        in_specs=[
            pl.BlockSpec((1, LANES), lambda k: (0, k)),
            pl.BlockSpec((1, LANES), lambda k: (0, k)),
            whole(face_u),
            whole(face_v),
            whole(flag),
            whole(sea),
            column(lons),
            column(HALO),
            column(HALO),
        ],
        out_specs=column(lons),
        scratch_shapes=[pltpu.VMEM((rows + 2, wide, LANES), jnp.float32)] * 2,
        compiler_params=pltpu.CompilerParams(vmem_limit_bytes=40 * 2**20),
        name="advect",
    )(speed_x, speed_y, face_u, face_v, flag, sea, field, left, right)


def source_kernel(field_ref, high_ref, low_ref, gain_ref, keep_ref, out_ref):
    comps = field_ref.shape[1]
    field = field_ref[...]
    field_high = field.astype(jnp.bfloat16)
    field_low = (field - field_high.astype(jnp.float32)).astype(jnp.bfloat16)

    def product(start):
        dims = (((1,), (1,)), ((), ()))
        dot = functools.partial(lax.dot_general, dimension_numbers=dims, preferred_element_type=jnp.float32)
        high = high_ref[start : start + comps, :]
        low = low_ref[start : start + comps, :]
        return dot(field_high, low) + dot(field_low, high) + dot(field_high, high)

    plus = product(0)
    minus = product(comps)
    gain = gain_ref[...]
    forcing = field * (field * (plus + minus) - 2.0 * plus * minus)
    update = gain * forcing / (1.0 + gain * (plus * plus + minus * minus))
    out_ref[...] = (field + update) * keep_ref[...]


def source(field, high, low, gain, keep):
    points, comps = field.shape
    tile = min(256, points)
    return pl.pallas_call(
        source_kernel,
        grid=(points // tile,),
        out_shape=jax.ShapeDtypeStruct(field.shape, jnp.float32),
        in_specs=[
            pl.BlockSpec((tile, comps), lambda p: (p, 0)),
            pl.BlockSpec(high.shape, lambda p: (0, 0)),
            pl.BlockSpec(low.shape, lambda p: (0, 0)),
            pl.BlockSpec((1, comps), lambda p: (0, 0)),
            pl.BlockSpec((tile, 1), lambda p: (p, 0)),
        ],
        out_specs=pl.BlockSpec((tile, comps), lambda p: (p, 0)),
        compiler_params=pltpu.CompilerParams(vmem_limit_bytes=56 * 2**20),
        name="source",
    )(field, high, low, gain, keep)


def body(
    spectrum, interp_plus, interp_minus, source_gain, current, sea_mask, limiter_flags, ice_cells
):
    bands = lax.axis_size("lat")
    ranks = lax.axis_size("comp")
    count = bands * ranks
    local_k, band_rows, lon_count = spectrum.shape
    comps = local_k * ranks
    rows = band_rows * bands
    lons = lon_count // count
    lat_rank = lax.axis_index("lat")
    comp_rank = lax.axis_index("comp")

    order = [
        band * ranks + (rank if band % 2 == 0 else ranks - 1 - rank)
        for band in range(bands)
        for rank in range(ranks)
    ]
    block = lat_rank * ranks + jnp.where(lat_rank % 2 == 0, comp_rank, ranks - 1 - comp_rank)

    def snake(blocks):
        parts = [
            blocks[band * ranks : (band + 1) * ranks] for band in range(bands)
        ]
        return jnp.concatenate([part if band % 2 == 0 else part[::-1] for band, part in enumerate(parts)])

    spread = snake(spectrum.reshape(local_k, band_rows, count, lons).transpose(2, 0, 1, 3))
    spread = spread.reshape(count, local_k, band_rows * lons)
    gathered = lax.all_to_all(spread, BOTH, split_axis=0, concat_axis=0, tiled=True)
    field = gathered.reshape(bands, comps, band_rows * lons).transpose(0, 2, 1)
    field = field.reshape(rows, lons, comps)

    statics = jnp.stack(
        [current[0], current[1], limiter_flags.astype(jnp.float32), sea_mask.astype(jnp.float32)]
    )
    statics = lax.all_gather(statics, "lat", axis=1, tiled=True)
    wide = lons + 2 * HALO
    ring = jnp.concatenate([statics[:, :, -HALO:], statics, statics[:, :, : HALO + 1]], axis=2)
    window = lax.dynamic_slice(ring, (0, 0, block * lons), (4, rows, wide + 1))
    drift_x, drift_y, flag, sea = window
    lanes = lambda plane: jnp.broadcast_to(plane[:, :, None], plane.shape + (LANES,))
    face_u = lanes(0.5 * (drift_x[:, :wide] + drift_x[:, 1:]))
    edged = jnp.pad(drift_y[:, :wide], ((1, 1), (0, 0)))
    face_v = lanes(0.5 * (edged[:-1] + edged[1:]))
    flag = lanes(jnp.pad(flag[:, :wide], ((0, 1), (0, 0))))
    sea = lanes(sea[:, :wide])
    speed_x, speed_y = speeds(jnp.arange(comps, dtype=jnp.int32))
    fixed = (speed_x, speed_y, face_u, face_v, flag, sea)

    cell = (
        jnp.arange(rows, dtype=jnp.int32)[:, None] * lon_count
        + block * lons
        + jnp.arange(lons, dtype=jnp.int32)[None, :]
    ).reshape(rows * lons)
    iced = jnp.any(cell[:, None] == ice_cells[None, :], axis=1)
    keep = jnp.where(iced, 1.0 - 0.6 * 1.0, 1.0).astype(jnp.float32)[:, None]

    weights = jnp.concatenate(
        [
            lax.all_gather(interp_plus, "lat", axis=0, tiled=True),
            lax.all_gather(interp_minus, "lat", axis=0, tiled=True),
        ]
    )
    rounded = lax.reduce_precision(weights, 8, 7)
    high = rounded.astype(jnp.bfloat16)
    low = (weights - rounded).astype(jnp.bfloat16)
    gain = source_gain[None, :]

    eastward = [(order[b], order[(b + 1) % count]) for b in range(count)]
    westward = [(order[(b + 1) % count], order[b]) for b in range(count)]
    for outer_step in range(OUTER):
        left = lax.ppermute(field[:, lons - HALO :], BOTH, eastward)
        right = lax.ppermute(field[:, :HALO], BOTH, westward)
        field = advect(field, left, right, fixed)
        field = source(field.reshape(rows * lons, comps), high, low, gain, keep)
        field = field.reshape(rows, lons, comps)

    spread = field.reshape(bands, band_rows * lons, comps).transpose(0, 2, 1)
    spread = spread.reshape(count, local_k, band_rows * lons)
    gathered = lax.all_to_all(spread, BOTH, split_axis=0, concat_axis=0, tiled=True)
    blocks = snake(gathered).reshape(count, local_k, band_rows, lons)
    return blocks.transpose(1, 2, 0, 3).reshape(local_k, band_rows, lon_count)


def solution(mesh):
    placed = (
        P("comp", "lat", None),
        P("lat", None),
        P("lat", None),
        P(),
        P(None, "lat", None),
        P("lat", None),
        P("lat", None),
        P(),
    )
    return jax.shard_map(
        body, mesh=mesh, in_specs=placed, out_specs=P("comp", "lat", None), check_vma=False
    )
```

```python
import functools

import jax
import jax.numpy as jnp
from jax import lax
from jax.experimental import pallas as pl
from jax.experimental.pallas import tpu as pltpu
from jax.sharding import PartitionSpec as P

ND = 36
NF = 32
OUTER = 2
SUB = 2
HALO = 2 * SUB
LANES = 128
BOTH = ("lat", "comp")


def speeds(index):
    direction = (index // NF).astype(jnp.float32)
    frequency = (index % NF).astype(jnp.float32)
    angle_dir = 2.0 * jnp.pi * (direction + 0.5) / ND
    magnitude = 0.35 * (0.5 + 0.5 * frequency / (NF - 1))
    return (magnitude * jnp.cos(angle_dir))[None, :], (magnitude * jnp.sin(angle_dir))[None, :]


def minmod(first, second):
    return jnp.maximum(jnp.minimum(first, second), 0.0) + jnp.minimum(jnp.maximum(first, second), 0.0)


def upwind(face, low, low_slope, high, high_slope):
    half = 0.5 - 0.5 * jnp.abs(face)
    return face * jnp.where(face >= 0.0, low + half * low_slope, high - half * high_slope)


def advect_kernel(
    cx_ref, cy_ref, uf_ref, vf_ref, flag_ref, sea_ref, field_ref, left_ref, right_ref, out_ref, first, second
):
    rows, lons, lanes = field_ref.shape
    wide = lons + 2 * HALO
    zero = jnp.zeros((wide, lanes), jnp.float32)
    first[:rows, :HALO, :] = left_ref[...]
    first[:rows, HALO : HALO + lons, :] = field_ref[...]
    first[:rows, HALO + lons :, :] = right_ref[...]
    for extra in range(2):
        first[rows + extra] = zero
        second[rows + extra] = zero
    speed_x = cx_ref[...]
    speed_y = cy_ref[...]

    def substep(source, store):
        top = source[0]
        below = source[1]
        step = below - top
        slope = flag_ref[0] * minmod(step, top)
        flux = upwind(speed_y + vf_ref[0], zero, zero, top, slope)

        def row(r, carry):
            here, south, step, slope, flux = carry
            beyond = source[r + 2]
            next_step = beyond - south
            next_slope = flag_ref[r + 1] * minmod(next_step, step)
            next_flux = upwind(speed_y + vf_ref[r + 1], here, slope, south, next_slope)
            east = pltpu.roll(here, wide - 1, 0)
            forward = east - here
            slope_x = flag_ref[r] * minmod(forward, pltpu.roll(forward, 1, 0))
            flux_x = upwind(
                speed_x + uf_ref[r], here, slope_x, east, pltpu.roll(slope_x, wide - 1, 0)
            )
            change_x = flux_x - pltpu.roll(flux_x, 1, 0)
            store(r, sea_ref[r] * (here - change_x - (next_flux - flux)))
            return south, beyond, next_step, next_slope, next_flux

        lax.fori_loop(0, rows, row, (top, below, step, slope, flux), unroll=2)

    def keep_second(r, value):
        second[r] = value

    def keep_out(r, value):
        out_ref[r] = value[HALO : HALO + lons]

    substep(first, keep_second)
    substep(second, keep_out)


def advect(field, left, right, fixed):
    speed_x, speed_y, face_u, face_v, flag, sea = fixed
    rows, lons, comps = field.shape
    wide = lons + 2 * HALO
    column = lambda height: pl.BlockSpec((rows, height, LANES), lambda k: (0, 0, k))
    whole = lambda array: pl.BlockSpec(array.shape, lambda k: (0, 0, 0))
    return pl.pallas_call(
        advect_kernel,
        grid=(comps // LANES,),
        out_shape=jax.ShapeDtypeStruct(field.shape, jnp.float32),
        in_specs=[
            pl.BlockSpec((1, LANES), lambda k: (0, k)),
            pl.BlockSpec((1, LANES), lambda k: (0, k)),
            whole(face_u),
            whole(face_v),
            whole(flag),
            whole(sea),
            column(lons),
            column(HALO),
            column(HALO),
        ],
        out_specs=column(lons),
        scratch_shapes=[pltpu.VMEM((rows + 2, wide, LANES), jnp.float32)] * 2,
        compiler_params=pltpu.CompilerParams(vmem_limit_bytes=40 * 2**20),
        name="advect",
    )(speed_x, speed_y, face_u, face_v, flag, sea, field, left, right)


def source_kernel(field_ref, high_ref, low_ref, gain_ref, keep_ref, out_ref):
    comps = field_ref.shape[1]
    field = field_ref[...]
    field_high = field.astype(jnp.bfloat16)
    field_low = (field - field_high.astype(jnp.float32)).astype(jnp.bfloat16)

    def product(start):
        dims = (((1,), (1,)), ((), ()))
        dot = functools.partial(lax.dot_general, dimension_numbers=dims, preferred_element_type=jnp.float32)
        high = high_ref[start : start + comps, :]
        low = low_ref[start : start + comps, :]
        return dot(field_high, low) + dot(field_low, high) + dot(field_high, high)

    plus = product(0)
    minus = product(comps)
    gain = gain_ref[...]
    forcing = field * (field * (plus + minus) - 2.0 * plus * minus)
    update = gain * forcing / (1.0 + gain * (plus * plus + minus * minus))
    out_ref[...] = (field + update) * keep_ref[...]


def source(field, high, low, gain, keep):
    points, comps = field.shape
    tile = min(256, points)
    return pl.pallas_call(
        source_kernel,
        grid=(points // tile,),
        out_shape=jax.ShapeDtypeStruct(field.shape, jnp.float32),
        in_specs=[
            pl.BlockSpec((tile, comps), lambda p: (p, 0)),
            pl.BlockSpec(high.shape, lambda p: (0, 0)),
            pl.BlockSpec(low.shape, lambda p: (0, 0)),
            pl.BlockSpec((1, comps), lambda p: (0, 0)),
            pl.BlockSpec((tile, 1), lambda p: (p, 0)),
        ],
        out_specs=pl.BlockSpec((tile, comps), lambda p: (p, 0)),
        compiler_params=pltpu.CompilerParams(vmem_limit_bytes=56 * 2**20),
        name="source",
    )(field, high, low, gain, keep)


def regroup(pieces, lane_group, width, moves):
    result = None
    for g, piece in enumerate(pieces):
        shift = ((g - moves[g]) * width) % LANES
        piece = pltpu.roll(piece, shift, 1) if shift else piece
        result = piece if result is None else jnp.where(lane_group == g, piece, result)
    return result


def split_kernel(order, width, field_ref, out_ref):
    group = LANES // width
    comps, rows, lons = field_ref.shape
    lane_group = lax.broadcasted_iota(jnp.int32, (comps, LANES), 1) // width
    for tile in range(lons // LANES):
        for band in range(rows // group):
            pieces = [
                field_ref[:, band * group + g, tile * LANES : (tile + 1) * LANES] for g in range(group)
            ]
            for part in range(group):
                out_ref[order[tile * group + part], :, band * LANES : (band + 1) * LANES] = regroup(
                    pieces, lane_group, width, [part] * group
                )


def join_kernel(order, width, blocks_ref, out_ref):
    group = LANES // width
    comps, rows, lons = out_ref.shape
    lane_group = lax.broadcasted_iota(jnp.int32, (comps, LANES), 1) // width
    for tile in range(lons // LANES):
        for band in range(rows // group):
            pieces = [
                blocks_ref[order[tile * group + part], :, band * LANES : (band + 1) * LANES]
                for part in range(group)
            ]
            for g in range(group):
                out_ref[:, band * group + g, tile * LANES : (tile + 1) * LANES] = regroup(
                    pieces, lane_group, width, [g] * group
                )


def tiled(shape, width):
    local_k, band_rows, lon_count = shape
    return LANES % width == 0 and band_rows % (LANES // width) == 0 and local_k % 8 == 0


def split(field, order, width):
    local_k, band_rows, lon_count = field.shape
    count = len(order)
    if not tiled(field.shape, width):
        parts = field.reshape(local_k, band_rows, count, width).transpose(2, 0, 1, 3)
        parts = jnp.stack([parts[order.index(d)] for d in range(count)])
        return parts.reshape(count, local_k, band_rows * width)
    return pl.pallas_call(
        functools.partial(split_kernel, order, width),
        grid=(local_k // 8,),
        out_shape=jax.ShapeDtypeStruct((count, local_k, band_rows * width), jnp.float32),
        in_specs=[pl.BlockSpec((8, band_rows, lon_count), lambda k: (k, 0, 0))],
        out_specs=pl.BlockSpec((count, 8, band_rows * width), lambda k: (0, k, 0)),
        name="split",
    )(field)


def join(blocks, order, shape, width):
    local_k, band_rows, lon_count = shape
    count = len(order)
    if not tiled(shape, width):
        parts = jnp.stack([blocks[d] for d in order]).reshape(count, local_k, band_rows, width)
        return parts.transpose(1, 2, 0, 3).reshape(shape)
    return pl.pallas_call(
        functools.partial(join_kernel, order, width),
        grid=(local_k // 8,),
        out_shape=jax.ShapeDtypeStruct(shape, jnp.float32),
        in_specs=[pl.BlockSpec((count, 8, band_rows * width), lambda k: (0, k, 0))],
        out_specs=pl.BlockSpec((8, band_rows, lon_count), lambda k: (k, 0, 0)),
        name="join",
    )(blocks)


def whole_maps(interp_plus, interp_minus, lat_rank, comp_rank, ranks):
    even = comp_rank % 2 == 0
    fetched = lax.ppermute(jnp.where(even, interp_plus, interp_minus), "lat", [(0, 1), (1, 0)])
    shared = lax.ppermute(fetched, "comp", [(i, i ^ 1) for i in range(ranks)])
    first = lat_rank == 0
    pieces = []
    for own, other in (
        (interp_plus, jnp.where(even, fetched, shared)),
        (interp_minus, jnp.where(even, shared, fetched)),
    ):
        pieces += [jnp.where(first, own, other), jnp.where(first, other, own)]
    return pieces


def body(
    spectrum, interp_plus, interp_minus, source_gain, current, sea_mask, limiter_flags, ice_cells
):
    bands = lax.axis_size("lat")
    ranks = lax.axis_size("comp")
    count = bands * ranks
    local_k, band_rows, lon_count = spectrum.shape
    comps = local_k * ranks
    rows = band_rows * bands
    lons = lon_count // count
    lat_rank = lax.axis_index("lat")
    comp_rank = lax.axis_index("comp")

    order = [
        band * ranks + (rank if band % 2 == 0 else ranks - 1 - rank)
        for band in range(bands)
        for rank in range(ranks)
    ]
    block = lat_rank * ranks + jnp.where(lat_rank % 2 == 0, comp_rank, ranks - 1 - comp_rank)

    spread = split(spectrum, order, lons)
    gathered = lax.all_to_all(spread, BOTH, split_axis=0, concat_axis=0, tiled=True)
    field = gathered.reshape(bands, comps, band_rows * lons).transpose(0, 2, 1)
    field = field.reshape(rows, lons, comps)

    statics = jnp.stack(
        [current[0], current[1], limiter_flags.astype(jnp.float32), sea_mask.astype(jnp.float32)]
    )
    statics = lax.all_gather(statics, "lat", axis=1, tiled=True)
    wide = lons + 2 * HALO
    ring = jnp.concatenate([statics[:, :, -HALO:], statics, statics[:, :, : HALO + 1]], axis=2)
    window = lax.dynamic_slice(ring, (0, 0, block * lons), (4, rows, wide + 1))
    drift_x, drift_y, flag, sea = window
    lanes = lambda plane: jnp.broadcast_to(plane[:, :, None], plane.shape + (LANES,))
    face_u = lanes(0.5 * (drift_x[:, :wide] + drift_x[:, 1:]))
    edged = jnp.pad(drift_y[:, :wide], ((1, 1), (0, 0)))
    face_v = lanes(0.5 * (edged[:-1] + edged[1:]))
    flag = lanes(jnp.pad(flag[:, :wide], ((0, 1), (0, 0))))
    sea = lanes(sea[:, :wide])
    speed_x, speed_y = speeds(jnp.arange(comps, dtype=jnp.int32))
    fixed = (speed_x, speed_y, face_u, face_v, flag, sea)

    cell = (
        jnp.arange(rows, dtype=jnp.int32)[:, None] * lon_count
        + block * lons
        + jnp.arange(lons, dtype=jnp.int32)[None, :]
    ).reshape(rows * lons)
    iced = jnp.any(cell[:, None] == ice_cells[None, :], axis=1)
    keep = jnp.where(iced, 1.0 - 0.6 * 1.0, 1.0).astype(jnp.float32)[:, None]

    pieces = whole_maps(interp_plus, interp_minus, lat_rank, comp_rank, ranks)
    rounded = [lax.reduce_precision(piece, 8, 7) for piece in pieces]
    high = jnp.concatenate([part.astype(jnp.bfloat16) for part in rounded])
    low = jnp.concatenate([(piece - part).astype(jnp.bfloat16) for piece, part in zip(pieces, rounded)])
    gain = source_gain[None, :]

    eastward = [(order[b], order[(b + 1) % count]) for b in range(count)]
    westward = [(order[(b + 1) % count], order[b]) for b in range(count)]
    for outer_step in range(OUTER):
        left = lax.ppermute(field[:, lons - HALO :], BOTH, eastward)
        right = lax.ppermute(field[:, :HALO], BOTH, westward)
        field = advect(field, left, right, fixed)
        field = source(field.reshape(rows * lons, comps), high, low, gain, keep)
        field = field.reshape(rows, lons, comps)

    spread = field.reshape(bands, band_rows * lons, comps).transpose(0, 2, 1)
    spread = spread.reshape(count, local_k, band_rows * lons)
    gathered = lax.all_to_all(spread, BOTH, split_axis=0, concat_axis=0, tiled=True)
    return join(gathered, order, spectrum.shape, lons)


def solution(mesh):
    placed = (
        P("comp", "lat", None),
        P("lat", None),
        P("lat", None),
        P(),
        P(None, "lat", None),
        P("lat", None),
        P("lat", None),
        P(),
    )
    return jax.shard_map(
        body, mesh=mesh, in_specs=placed, out_specs=P("comp", "lat", None), check_vma=False
    )
```

```python
import functools

import jax
import jax.numpy as jnp
from jax import lax
from jax.experimental import pallas as pl
from jax.experimental.pallas import tpu as pltpu
from jax.sharding import PartitionSpec as P

ND = 36
NF = 32
OUTER = 2
SUB = 2
HALO = 2 * SUB
LANES = 128
BOTH = ("lat", "comp")


def speeds(index):
    direction = (index // NF).astype(jnp.float32)
    frequency = (index % NF).astype(jnp.float32)
    angle_dir = 2.0 * jnp.pi * (direction + 0.5) / ND
    magnitude = 0.35 * (0.5 + 0.5 * frequency / (NF - 1))
    return (magnitude * jnp.cos(angle_dir))[None, :], (magnitude * jnp.sin(angle_dir))[None, :]


def minmod(first, second):
    return jnp.maximum(jnp.minimum(first, second), 0.0) + jnp.minimum(jnp.maximum(first, second), 0.0)


def upwind(face, low, low_slope, high, high_slope):
    half = 0.5 - 0.5 * jnp.abs(face)
    return face * jnp.where(face >= 0.0, low + half * low_slope, high - half * high_slope)


def advect_kernel(
    cx_ref, cy_ref, uf_ref, vf_ref, flag_ref, sea_ref, field_ref, left_ref, right_ref, out_ref, first, second
):
    rows, lons, lanes = field_ref.shape
    wide = lons + 2 * HALO
    zero = jnp.zeros((wide, lanes), jnp.float32)
    first[:rows, :HALO, :] = left_ref[...]
    first[:rows, HALO : HALO + lons, :] = field_ref[...]
    first[:rows, HALO + lons :, :] = right_ref[...]
    for extra in range(2):
        first[rows + extra] = zero
        second[rows + extra] = zero
    speed_x = cx_ref[...]
    speed_y = cy_ref[...]

    def substep(source, store):
        top = source[0]
        below = source[1]
        step = below - top
        slope = flag_ref[0] * minmod(step, top)
        flux = upwind(speed_y + vf_ref[0], zero, zero, top, slope)

        def row(r, carry):
            here, south, step, slope, flux = carry
            beyond = source[r + 2]
            next_step = beyond - south
            next_slope = flag_ref[r + 1] * minmod(next_step, step)
            next_flux = upwind(speed_y + vf_ref[r + 1], here, slope, south, next_slope)
            east = pltpu.roll(here, wide - 1, 0)
            forward = east - here
            slope_x = flag_ref[r] * minmod(forward, pltpu.roll(forward, 1, 0))
            flux_x = upwind(
                speed_x + uf_ref[r], here, slope_x, east, pltpu.roll(slope_x, wide - 1, 0)
            )
            change_x = flux_x - pltpu.roll(flux_x, 1, 0)
            store(r, sea_ref[r] * (here - change_x - (next_flux - flux)))
            return south, beyond, next_step, next_slope, next_flux

        lax.fori_loop(0, rows, row, (top, below, step, slope, flux), unroll=2)

    def keep_second(r, value):
        second[r] = value

    def keep_out(r, value):
        out_ref[r] = value[HALO : HALO + lons]

    substep(first, keep_second)
    substep(second, keep_out)


def advect(field, left, right, fixed):
    speed_x, speed_y, face_u, face_v, flag, sea = fixed
    rows, lons, comps = field.shape
    wide = lons + 2 * HALO
    column = lambda height: pl.BlockSpec((rows, height, LANES), lambda k: (0, 0, k))
    whole = lambda array: pl.BlockSpec(array.shape, lambda k: (0, 0, 0))
    return pl.pallas_call(
        advect_kernel,
        grid=(comps // LANES,),
        out_shape=jax.ShapeDtypeStruct(field.shape, jnp.float32),
        in_specs=[
            pl.BlockSpec((1, LANES), lambda k: (0, k)),
            pl.BlockSpec((1, LANES), lambda k: (0, k)),
            whole(face_u),
            whole(face_v),
            whole(flag),
            whole(sea),
            column(lons),
            column(HALO),
            column(HALO),
        ],
        out_specs=column(lons),
        scratch_shapes=[pltpu.VMEM((rows + 2, wide, LANES), jnp.float32)] * 2,
        compiler_params=pltpu.CompilerParams(vmem_limit_bytes=40 * 2**20),
        name="advect",
    )(speed_x, speed_y, face_u, face_v, flag, sea, field, left, right)


def source_kernel(turned, field_ref, high_ref, low_ref, gain_ref, keep_ref, out_ref):
    comps = field_ref.shape[1]
    field = field_ref[...]
    field_high = field.astype(jnp.bfloat16)
    field_low = (field - field_high.astype(jnp.float32)).astype(jnp.bfloat16)

    def product(start):
        dims = (((1,), (1,)), ((), ()))
        dot = functools.partial(lax.dot_general, dimension_numbers=dims, preferred_element_type=jnp.float32)
        high = high_ref[start : start + comps, :]
        low = low_ref[start : start + comps, :]
        return dot(field_high, low) + dot(field_low, high) + dot(field_high, high)

    plus = product(0)
    minus = product(comps)
    gain = gain_ref[...]
    forcing = field * (field * (plus + minus) - 2.0 * plus * minus)
    update = gain * forcing / (1.0 + gain * (plus * plus + minus * minus))
    result = (field + update) * keep_ref[...]
    if turned:
        out_ref[0] = result.T
    else:
        out_ref[...] = result


def source(field, high, low, gain, keep, bands=0, half=0):
    points, comps = field.shape
    if bands:
        tile = points // (2 * bands)
        grid = (bands,)
        place = lambda p: (2 * p + half, 0)
        result = jax.ShapeDtypeStruct((bands, comps, tile), jnp.float32)
        out_spec = pl.BlockSpec((1, comps, tile), lambda p: (p, 0, 0))
    else:
        tile = min(256, points)
        grid = (points // tile,)
        place = lambda p: (p, 0)
        result = jax.ShapeDtypeStruct(field.shape, jnp.float32)
        out_spec = pl.BlockSpec((tile, comps), place)
    work = grid[0] * tile * comps
    return pl.pallas_call(
        functools.partial(source_kernel, bands > 0),
        grid=grid,
        out_shape=result,
        in_specs=[
            pl.BlockSpec((tile, comps), place),
            pl.BlockSpec(high.shape, lambda p: (0, 0)),
            pl.BlockSpec(low.shape, lambda p: (0, 0)),
            pl.BlockSpec((1, comps), lambda p: (0, 0)),
            pl.BlockSpec((tile, 1), place),
        ],
        out_specs=out_spec,
        compiler_params=pltpu.CompilerParams(vmem_limit_bytes=56 * 2**20),
        cost_estimate=pl.CostEstimate(
            flops=12 * work * comps, bytes_accessed=8 * work + 8 * comps * comps, transcendentals=0
        ),
        name="source",
    )(field, high, low, gain, keep)


def regroup(pieces, lane_group, width, moves):
    result = None
    for g, piece in enumerate(pieces):
        shift = ((g - moves[g]) * width) % LANES
        piece = pltpu.roll(piece, shift, 1) if shift else piece
        result = piece if result is None else jnp.where(lane_group == g, piece, result)
    return result


def split_kernel(order, width, field_ref, out_ref):
    group = LANES // width
    comps, rows, lons = field_ref.shape
    lane_group = lax.broadcasted_iota(jnp.int32, (comps, LANES), 1) // width
    for tile in range(lons // LANES):
        for band in range(rows // group):
            pieces = [
                field_ref[:, band * group + g, tile * LANES : (tile + 1) * LANES] for g in range(group)
            ]
            for part in range(group):
                out_ref[order[tile * group + part], :, band * LANES : (band + 1) * LANES] = regroup(
                    pieces, lane_group, width, [part] * group
                )


def join_kernel(order, width, upper_ref, lower_ref, out_ref):
    group = LANES // width
    comps, rows, lons = out_ref.shape
    lane_group = lax.broadcasted_iota(jnp.int32, (comps, LANES), 1) // width
    for tile in range(lons // LANES):
        for band in range(rows // group):
            middle = rows // group // 2
            half_ref = upper_ref if band < middle else lower_ref
            start = (band % middle) * LANES
            pieces = [
                half_ref[order[tile * group + part], :, start : start + LANES]
                for part in range(group)
            ]
            for g in range(group):
                out_ref[:, band * group + g, tile * LANES : (tile + 1) * LANES] = regroup(
                    pieces, lane_group, width, [g] * group
                )


def tiled(shape, width):
    local_k, band_rows, lon_count = shape
    return LANES % width == 0 and band_rows % (2 * LANES // width) == 0 and local_k % 8 == 0


def split(field, order, width):
    local_k, band_rows, lon_count = field.shape
    count = len(order)
    if not tiled(field.shape, width):
        parts = field.reshape(local_k, band_rows, count, width).transpose(2, 0, 1, 3)
        parts = jnp.stack([parts[order.index(d)] for d in range(count)])
        return parts.reshape(count, local_k, band_rows * width)
    return pl.pallas_call(
        functools.partial(split_kernel, order, width),
        grid=(local_k // 8,),
        out_shape=jax.ShapeDtypeStruct((count, local_k, band_rows * width), jnp.float32),
        in_specs=[pl.BlockSpec((8, band_rows, lon_count), lambda k: (k, 0, 0))],
        out_specs=pl.BlockSpec((count, 8, band_rows * width), lambda k: (0, k, 0)),
        name="split",
    )(field)


def join(upper, lower, order, shape, width):
    local_k, band_rows, lon_count = shape
    count = len(order)
    if not tiled(shape, width):
        blocks = jnp.concatenate([upper, lower], axis=2)
        parts = jnp.stack([blocks[d] for d in order]).reshape(count, local_k, band_rows, width)
        return parts.transpose(1, 2, 0, 3).reshape(shape)
    return pl.pallas_call(
        functools.partial(join_kernel, order, width),
        grid=(local_k // 8,),
        out_shape=jax.ShapeDtypeStruct(shape, jnp.float32),
        in_specs=[pl.BlockSpec((count, 8, band_rows * width // 2), lambda k: (0, k, 0))] * 2,
        out_specs=pl.BlockSpec((8, band_rows, lon_count), lambda k: (k, 0, 0)),
        name="join",
    )(upper, lower)


def maps_kernel(rank_ref, plus_ref, minus_ref, fetched_ref, shared_ref, high_ref, low_ref):
    lat_rank = rank_ref[0]
    even = rank_ref[1] == 0

    def put(quarter, piece_ref):
        piece = piece_ref[...]
        rounded = piece.astype(jnp.bfloat16)
        high_ref[quarter] = rounded
        low_ref[quarter] = (piece - rounded.astype(jnp.float32)).astype(jnp.bfloat16)

    put(lat_rank, plus_ref)
    put(2 + lat_rank, minus_ref)

    @pl.when(even)
    def _():
        put(1 - lat_rank, fetched_ref)
        put(3 - lat_rank, shared_ref)

    @pl.when(jnp.logical_not(even))
    def _():
        put(1 - lat_rank, shared_ref)
        put(3 - lat_rank, fetched_ref)


def whole_maps(interp_plus, interp_minus, fetched, lat_rank, comp_rank, ranks):
    shared = lax.ppermute(fetched, "comp", [(i, i ^ 1) for i in range(ranks)])
    rows, comps = interp_plus.shape
    tile = rows // 6
    result = jax.ShapeDtypeStruct((4, rows, comps), jnp.bfloat16)
    high, low = pl.pallas_call(
        maps_kernel,
        grid_spec=pltpu.PrefetchScalarGridSpec(
            num_scalar_prefetch=1,
            grid=(rows // tile,),
            in_specs=[pl.BlockSpec((tile, comps), lambda p, rank: (p, 0))] * 4,
            out_specs=[pl.BlockSpec((4, tile, comps), lambda p, rank: (0, p, 0))] * 2,
        ),
        out_shape=[result, result],
        compiler_params=pltpu.CompilerParams(vmem_limit_bytes=24 * 2**20),
        name="maps",
    )(jnp.stack([lat_rank, comp_rank % 2]), interp_plus, interp_minus, fetched, shared)
    return high.reshape(4 * rows, comps), low.reshape(4 * rows, comps)


def body(
    spectrum, interp_plus, interp_minus, source_gain, current, sea_mask, limiter_flags, ice_cells
):
    bands = lax.axis_size("lat")
    ranks = lax.axis_size("comp")
    count = bands * ranks
    local_k, band_rows, lon_count = spectrum.shape
    comps = local_k * ranks
    rows = band_rows * bands
    lons = lon_count // count
    lat_rank = lax.axis_index("lat")
    comp_rank = lax.axis_index("comp")

    order = [
        band * ranks + (rank if band % 2 == 0 else ranks - 1 - rank)
        for band in range(bands)
        for rank in range(ranks)
    ]
    block = lat_rank * ranks + jnp.where(lat_rank % 2 == 0, comp_rank, ranks - 1 - comp_rank)

    send = jnp.where(comp_rank % 2 == 0, interp_plus, interp_minus)
    spectrum, send = lax.optimization_barrier((spectrum, send))
    fetched = lax.ppermute(send, "lat", [(0, 1), (1, 0)])
    spread = split(spectrum, order, lons)
    gathered = lax.all_to_all(spread, BOTH, split_axis=0, concat_axis=0, tiled=True)
    field = gathered.reshape(bands, comps, band_rows * lons).transpose(0, 2, 1)
    field = field.reshape(rows, lons, comps)

    statics = jnp.stack(
        [current[0], current[1], limiter_flags.astype(jnp.float32), sea_mask.astype(jnp.float32)]
    )
    statics = lax.all_gather(statics, "lat", axis=1, tiled=True)
    wide = lons + 2 * HALO
    ring = jnp.concatenate([statics[:, :, -HALO:], statics, statics[:, :, : HALO + 1]], axis=2)
    window = lax.dynamic_slice(ring, (0, 0, block * lons), (4, rows, wide + 1))
    drift_x, drift_y, flag, sea = window
    lanes = lambda plane: jnp.broadcast_to(plane[:, :, None], plane.shape + (LANES,))
    face_u = lanes(0.5 * (drift_x[:, :wide] + drift_x[:, 1:]))
    edged = jnp.pad(drift_y[:, :wide], ((1, 1), (0, 0)))
    face_v = lanes(0.5 * (edged[:-1] + edged[1:]))
    flag = lanes(jnp.pad(flag[:, :wide], ((0, 1), (0, 0))))
    sea = lanes(sea[:, :wide])
    speed_x, speed_y = speeds(jnp.arange(comps, dtype=jnp.int32))
    fixed = (speed_x, speed_y, face_u, face_v, flag, sea)

    cell = (
        jnp.arange(rows, dtype=jnp.int32)[:, None] * lon_count
        + block * lons
        + jnp.arange(lons, dtype=jnp.int32)[None, :]
    ).reshape(rows * lons)
    iced = jnp.any(cell[:, None] == ice_cells[None, :], axis=1)
    keep = jnp.where(iced, 1.0 - 0.6 * 1.0, 1.0).astype(jnp.float32)[:, None]

    high, low = whole_maps(interp_plus, interp_minus, fetched, lat_rank, comp_rank, ranks)
    gain = source_gain[None, :]

    eastward = [(order[b], order[(b + 1) % count]) for b in range(count)]
    westward = [(order[(b + 1) % count], order[b]) for b in range(count)]
    for outer_step in range(OUTER):
        left = lax.ppermute(field[:, lons - HALO :], BOTH, eastward)
        right = lax.ppermute(field[:, :HALO], BOTH, westward)
        field = advect(field, left, right, fixed)
        field = field.reshape(rows * lons, comps)
        if outer_step < OUTER - 1:
            field = source(field, high, low, gain, keep).reshape(rows, lons, comps)

    halves = []
    for half in range(2):
        spread = source(field, high, low, gain, keep, bands, half)
        spread = spread.reshape(count, local_k, band_rows * lons // 2)
        halves.append(lax.all_to_all(spread, BOTH, split_axis=0, concat_axis=0, tiled=True))
    return join(halves[0], halves[1], order, spectrum.shape, lons)


def solution(mesh):
    placed = (
        P("comp", "lat", None),
        P("lat", None),
        P("lat", None),
        P(),
        P(None, "lat", None),
        P("lat", None),
        P("lat", None),
        P(),
    )
    return jax.shard_map(
        body, mesh=mesh, in_specs=placed, out_specs=P("comp", "lat", None), check_vma=False
    )
```

```python
import functools

import jax
import jax.numpy as jnp
from jax import lax
from jax.experimental import pallas as pl
from jax.experimental.pallas import tpu as pltpu
from jax.sharding import PartitionSpec as P

ND = 36
NF = 32
OUTER = 2
SUB = 2
HALO = 2 * SUB
LANES = 128
BOTH = ("lat", "comp")


def speeds(index):
    direction = (index // NF).astype(jnp.float32)
    frequency = (index % NF).astype(jnp.float32)
    angle_dir = 2.0 * jnp.pi * (direction + 0.5) / ND
    magnitude = 0.35 * (0.5 + 0.5 * frequency / (NF - 1))
    return (magnitude * jnp.cos(angle_dir))[None, :], (magnitude * jnp.sin(angle_dir))[None, :]


def minmod(first, second):
    return jnp.maximum(jnp.minimum(first, second), 0.0) + jnp.minimum(jnp.maximum(first, second), 0.0)


def upwind(face, low, low_slope, high, high_slope):
    half = 0.5 - 0.5 * jnp.abs(face)
    return face * jnp.where(face >= 0.0, low + half * low_slope, high - half * high_slope)


def advect_kernel(
    cx_ref, cy_ref, uf_ref, vf_ref, flag_ref, sea_ref, field_ref, left_ref, right_ref, out_ref, first, second
):
    rows, lons, lanes = field_ref.shape
    wide = lons + 2 * HALO
    zero = jnp.zeros((wide, lanes), jnp.float32)
    first[:rows, :HALO, :] = left_ref[...]
    first[:rows, HALO : HALO + lons, :] = field_ref[...]
    first[:rows, HALO + lons :, :] = right_ref[...]
    for extra in range(2):
        first[rows + extra] = zero
        second[rows + extra] = zero
    speed_x = cx_ref[...]
    speed_y = cy_ref[...]

    def substep(source, store):
        top = source[0]
        below = source[1]
        step = below - top
        slope = flag_ref[0] * minmod(step, top)
        flux = upwind(speed_y + vf_ref[0], zero, zero, top, slope)

        def row(r, carry):
            here, south, step, slope, flux = carry
            beyond = source[r + 2]
            next_step = beyond - south
            next_slope = flag_ref[r + 1] * minmod(next_step, step)
            next_flux = upwind(speed_y + vf_ref[r + 1], here, slope, south, next_slope)
            east = pltpu.roll(here, wide - 1, 0)
            forward = east - here
            slope_x = flag_ref[r] * minmod(forward, pltpu.roll(forward, 1, 0))
            flux_x = upwind(
                speed_x + uf_ref[r], here, slope_x, east, pltpu.roll(slope_x, wide - 1, 0)
            )
            change_x = flux_x - pltpu.roll(flux_x, 1, 0)
            store(r, sea_ref[r] * (here - change_x - (next_flux - flux)))
            return south, beyond, next_step, next_slope, next_flux

        lax.fori_loop(0, rows, row, (top, below, step, slope, flux), unroll=2)

    def keep_second(r, value):
        second[r] = value

    def keep_out(r, value):
        out_ref[r] = value[HALO : HALO + lons]

    substep(first, keep_second)
    substep(second, keep_out)


def advect(field, left, right, fixed):
    speed_x, speed_y, face_u, face_v, flag, sea = fixed
    rows, lons, comps = field.shape
    wide = lons + 2 * HALO
    column = lambda height: pl.BlockSpec((rows, height, LANES), lambda k: (0, 0, k))
    whole = lambda array: pl.BlockSpec(array.shape, lambda k: (0, 0, 0))
    return pl.pallas_call(
        advect_kernel,
        grid=(comps // LANES,),
        out_shape=jax.ShapeDtypeStruct(field.shape, jnp.float32),
        in_specs=[
            pl.BlockSpec((1, LANES), lambda k: (0, k)),
            pl.BlockSpec((1, LANES), lambda k: (0, k)),
            whole(face_u),
            whole(face_v),
            whole(flag),
            whole(sea),
            column(lons),
            column(HALO),
            column(HALO),
        ],
        out_specs=column(lons),
        scratch_shapes=[pltpu.VMEM((rows + 2, wide, LANES), jnp.float32)] * 2,
        compiler_params=pltpu.CompilerParams(vmem_limit_bytes=40 * 2**20),
        name="advect",
    )(speed_x, speed_y, face_u, face_v, flag, sea, field, left, right)


def source_kernel(turned, field_ref, high_ref, low_ref, gain_ref, keep_ref, out_ref):
    comps = field_ref.shape[1]
    field = field_ref[...]
    field_high = field.astype(jnp.bfloat16)
    field_low = (field - field_high.astype(jnp.float32)).astype(jnp.bfloat16)

    def product(start):
        dims = (((1,), (1,)), ((), ()))
        dot = functools.partial(lax.dot_general, dimension_numbers=dims, preferred_element_type=jnp.float32)
        high = high_ref[start : start + comps, :]
        low = low_ref[start : start + comps, :]
        return dot(field_high, low) + dot(field_low, high) + dot(field_high, high)

    plus = product(0)
    minus = product(comps)
    gain = gain_ref[...]
    forcing = field * (field * (plus + minus) - 2.0 * plus * minus)
    update = gain * forcing / (1.0 + gain * (plus * plus + minus * minus))
    result = (field + update) * keep_ref[...]
    if turned:
        out_ref[0] = result.T
    else:
        out_ref[...] = result


def source(field, high, low, gain, keep, bands=0, half=0):
    points, comps = field.shape
    if bands:
        tile = points // (2 * bands)
        grid = (bands,)
        place = lambda p: (2 * p + half, 0)
        result = jax.ShapeDtypeStruct((bands, comps, tile), jnp.float32)
        out_spec = pl.BlockSpec((1, comps, tile), lambda p: (p, 0, 0))
    else:
        tile = min(512, points)
        grid = (points // tile,)
        place = lambda p: (p, 0)
        result = jax.ShapeDtypeStruct(field.shape, jnp.float32)
        out_spec = pl.BlockSpec((tile, comps), place)
    work = grid[0] * tile * comps
    return pl.pallas_call(
        functools.partial(source_kernel, bands > 0),
        grid=grid,
        out_shape=result,
        in_specs=[
            pl.BlockSpec((tile, comps), place),
            pl.BlockSpec(high.shape, lambda p: (0, 0)),
            pl.BlockSpec(low.shape, lambda p: (0, 0)),
            pl.BlockSpec((1, comps), lambda p: (0, 0)),
            pl.BlockSpec((tile, 1), place),
        ],
        out_specs=out_spec,
        compiler_params=pltpu.CompilerParams(vmem_limit_bytes=56 * 2**20),
        cost_estimate=pl.CostEstimate(
            flops=12 * work * comps, bytes_accessed=8 * work + 8 * comps * comps, transcendentals=0
        ),
        name="source",
    )(field, high, low, gain, keep)


def regroup(pieces, lane_group, width, moves):
    result = None
    for g, piece in enumerate(pieces):
        shift = ((g - moves[g]) * width) % LANES
        piece = pltpu.roll(piece, shift, 1) if shift else piece
        result = piece if result is None else jnp.where(lane_group == g, piece, result)
    return result


def split_kernel(order, width, field_ref, out_ref):
    group = LANES // width
    comps, rows, lons = field_ref.shape
    lane_group = lax.broadcasted_iota(jnp.int32, (comps, LANES), 1) // width
    for tile in range(lons // LANES):
        for band in range(rows // group):
            pieces = [
                field_ref[:, band * group + g, tile * LANES : (tile + 1) * LANES] for g in range(group)
            ]
            for part in range(group):
                out_ref[order[tile * group + part], :, band * LANES : (band + 1) * LANES] = regroup(
                    pieces, lane_group, width, [part] * group
                )


def join_kernel(order, width, upper_ref, lower_ref, out_ref):
    group = LANES // width
    comps, rows, lons = out_ref.shape
    lane_group = lax.broadcasted_iota(jnp.int32, (comps, LANES), 1) // width
    for tile in range(lons // LANES):
        for band in range(rows // group):
            middle = rows // group // 2
            half_ref = upper_ref if band < middle else lower_ref
            start = (band % middle) * LANES
            pieces = [
                half_ref[order[tile * group + part], :, start : start + LANES]
                for part in range(group)
            ]
            for g in range(group):
                out_ref[:, band * group + g, tile * LANES : (tile + 1) * LANES] = regroup(
                    pieces, lane_group, width, [g] * group
                )


def tiled(shape, width):
    local_k, band_rows, lon_count = shape
    return LANES % width == 0 and band_rows % (2 * LANES // width) == 0 and local_k % 8 == 0


def split(field, order, width):
    local_k, band_rows, lon_count = field.shape
    count = len(order)
    if not tiled(field.shape, width):
        parts = field.reshape(local_k, band_rows, count, width).transpose(2, 0, 1, 3)
        parts = jnp.stack([parts[order.index(d)] for d in range(count)])
        return parts.reshape(count, local_k, band_rows * width)
    return pl.pallas_call(
        functools.partial(split_kernel, order, width),
        grid=(local_k // 8,),
        out_shape=jax.ShapeDtypeStruct((count, local_k, band_rows * width), jnp.float32),
        in_specs=[pl.BlockSpec((8, band_rows, lon_count), lambda k: (k, 0, 0))],
        out_specs=pl.BlockSpec((count, 8, band_rows * width), lambda k: (0, k, 0)),
        name="split",
    )(field)


def join(upper, lower, order, shape, width):
    local_k, band_rows, lon_count = shape
    count = len(order)
    if not tiled(shape, width):
        blocks = jnp.concatenate([upper, lower], axis=2)
        parts = jnp.stack([blocks[d] for d in order]).reshape(count, local_k, band_rows, width)
        return parts.transpose(1, 2, 0, 3).reshape(shape)
    return pl.pallas_call(
        functools.partial(join_kernel, order, width),
        grid=(local_k // 8,),
        out_shape=jax.ShapeDtypeStruct(shape, jnp.float32),
        in_specs=[pl.BlockSpec((count, 8, band_rows * width // 2), lambda k: (0, k, 0))] * 2,
        out_specs=pl.BlockSpec((8, band_rows, lon_count), lambda k: (k, 0, 0)),
        name="join",
    )(upper, lower)


def maps_kernel(rank_ref, plus_ref, minus_ref, fetched_ref, shared_ref, high_ref, low_ref):
    lat_rank = rank_ref[0]
    even = rank_ref[1] == 0

    def put(quarter, piece_ref):
        piece = piece_ref[...]
        rounded = piece.astype(jnp.bfloat16)
        high_ref[quarter] = rounded
        low_ref[quarter] = (piece - rounded.astype(jnp.float32)).astype(jnp.bfloat16)

    put(lat_rank, plus_ref)
    put(2 + lat_rank, minus_ref)

    @pl.when(even)
    def _():
        put(1 - lat_rank, fetched_ref)
        put(3 - lat_rank, shared_ref)

    @pl.when(jnp.logical_not(even))
    def _():
        put(1 - lat_rank, shared_ref)
        put(3 - lat_rank, fetched_ref)


def whole_maps(interp_plus, interp_minus, fetched, lat_rank, comp_rank, ranks):
    shared = lax.ppermute(fetched, "comp", [(i, i ^ 1) for i in range(ranks)])
    rows, comps = interp_plus.shape
    tile = rows // 6
    result = jax.ShapeDtypeStruct((4, rows, comps), jnp.bfloat16)
    high, low = pl.pallas_call(
        maps_kernel,
        grid_spec=pltpu.PrefetchScalarGridSpec(
            num_scalar_prefetch=1,
            grid=(rows // tile,),
            in_specs=[pl.BlockSpec((tile, comps), lambda p, rank: (p, 0))] * 4,
            out_specs=[pl.BlockSpec((4, tile, comps), lambda p, rank: (0, p, 0))] * 2,
        ),
        out_shape=[result, result],
        compiler_params=pltpu.CompilerParams(vmem_limit_bytes=24 * 2**20),
        name="maps",
    )(jnp.stack([lat_rank, comp_rank % 2]), interp_plus, interp_minus, fetched, shared)
    return high.reshape(4 * rows, comps), low.reshape(4 * rows, comps)


def body(
    spectrum, interp_plus, interp_minus, source_gain, current, sea_mask, limiter_flags, ice_cells
):
    bands = lax.axis_size("lat")
    ranks = lax.axis_size("comp")
    count = bands * ranks
    local_k, band_rows, lon_count = spectrum.shape
    comps = local_k * ranks
    rows = band_rows * bands
    lons = lon_count // count
    lat_rank = lax.axis_index("lat")
    comp_rank = lax.axis_index("comp")

    order = [
        band * ranks + (rank if band % 2 == 0 else ranks - 1 - rank)
        for band in range(bands)
        for rank in range(ranks)
    ]
    block = lat_rank * ranks + jnp.where(lat_rank % 2 == 0, comp_rank, ranks - 1 - comp_rank)

    send = jnp.where(comp_rank % 2 == 0, interp_plus, interp_minus)
    spectrum, send = lax.optimization_barrier((spectrum, send))
    fetched = lax.ppermute(send, "lat", [(0, 1), (1, 0)])
    spread = split(spectrum, order, lons)
    gathered = lax.all_to_all(spread, BOTH, split_axis=0, concat_axis=0, tiled=True)
    field = gathered.reshape(bands, comps, band_rows * lons).transpose(0, 2, 1)
    field = field.reshape(rows, lons, comps)

    statics = jnp.stack(
        [current[0], current[1], limiter_flags.astype(jnp.float32), sea_mask.astype(jnp.float32)]
    )
    beside = lax.ppermute(statics, "lat", [(0, 1), (1, 0)])
    first = lat_rank == 0
    statics = jnp.concatenate(
        [jnp.where(first, statics, beside), jnp.where(first, beside, statics)], axis=1
    )
    wide = lons + 2 * HALO
    ring = jnp.concatenate([statics[:, :, -HALO:], statics, statics[:, :, : HALO + 1]], axis=2)
    window = lax.dynamic_slice(ring, (0, 0, block * lons), (4, rows, wide + 1))
    drift_x, drift_y, flag, sea = window
    lanes = lambda plane: jnp.broadcast_to(plane[:, :, None], plane.shape + (LANES,))
    face_u = lanes(0.5 * (drift_x[:, :wide] + drift_x[:, 1:]))
    edged = jnp.pad(drift_y[:, :wide], ((1, 1), (0, 0)))
    face_v = lanes(0.5 * (edged[:-1] + edged[1:]))
    flag = lanes(jnp.pad(flag[:, :wide], ((0, 1), (0, 0))))
    sea = lanes(sea[:, :wide])
    speed_x, speed_y = speeds(jnp.arange(comps, dtype=jnp.int32))
    fixed = (speed_x, speed_y, face_u, face_v, flag, sea)

    cell = (
        jnp.arange(rows, dtype=jnp.int32)[:, None] * lon_count
        + block * lons
        + jnp.arange(lons, dtype=jnp.int32)[None, :]
    ).reshape(rows * lons)
    iced = jnp.any(cell[:, None] == ice_cells[None, :], axis=1)
    keep = jnp.where(iced, 1.0 - 0.6 * 1.0, 1.0).astype(jnp.float32)[:, None]

    high, low = whole_maps(interp_plus, interp_minus, fetched, lat_rank, comp_rank, ranks)
    gain = source_gain[None, :]

    eastward = [(order[b], order[(b + 1) % count]) for b in range(count)]
    westward = [(order[(b + 1) % count], order[b]) for b in range(count)]
    for outer_step in range(OUTER):
        left = lax.ppermute(field[:, lons - HALO :], BOTH, eastward)
        right = lax.ppermute(field[:, :HALO], BOTH, westward)
        field = advect(field, left, right, fixed)
        field = field.reshape(rows * lons, comps)
        if outer_step < OUTER - 1:
            field = source(field, high, low, gain, keep).reshape(rows, lons, comps)

    halves = []
    for half in range(2):
        spread = source(field, high, low, gain, keep, bands, half)
        spread = spread.reshape(count, local_k, band_rows * lons // 2)
        halves.append(lax.all_to_all(spread, BOTH, split_axis=0, concat_axis=0, tiled=True))
    return join(halves[0], halves[1], order, spectrum.shape, lons)


def solution(mesh):
    placed = (
        P("comp", "lat", None),
        P("lat", None),
        P("lat", None),
        P(),
        P(None, "lat", None),
        P("lat", None),
        P("lat", None),
        P(),
    )
    return jax.shard_map(
        body, mesh=mesh, in_specs=placed, out_specs=P("comp", "lat", None), check_vma=False
    )
```
